32 devices in a mesh: rep: 4 (over y, x), shard: 8 (over z, core).
Axes of the slice: x: 2, y: 2, z: 4, core: 2. Of those that a mesh axis runs over, the one named last changes fastest.
Arguments:
- inner_weights: float32 [4, 2, 512, 512], P('rep', None, 'shard'), may hold values from -6 to 6
- first_moment: float32 [4, 2, 512, 512], P('rep', None, 'shard'), may hold values from -1 to 1
- second_moment: float32 [4, 2, 512, 512], P('rep', None, 'shard'), may hold values from 0 to 1, as said below
- outer_weights: float32 [2, 512, 512], P(None, 'shard'), may hold values from -6 to 6
- outer_velocity: float32 [2, 512, 512], P(None, 'shard'), may hold values from -3 to 3
- tokens: bfloat16 [4, 2, 4096, 512], P('rep', None, 'shard'), may hold values from -6 to 6
- targets: bfloat16 [4, 2, 4096, 2, 512], P('rep', None, 'shard'), may hold values from -25 to 25
- step_count: int32 [1], replicated, may hold values from 10 to 39
- first_fragment: int32 [1], replicated, may hold values from 0 to 1
Outputs:
- new_outer: float32 [2, 512, 512], P(None, 'shard')
- new_inner: float32 [4, 2, 512, 512], P('rep', None, 'shard')
The draws below stay inside these ranges and needn't reach their ends.
Inputs may be any that keep to these rules, and one draw needn't show every extreme that they name: `second_moment`: positive.
All inputs are finite; a program needn't handle non-finite values.
Results may differ from the reference program's by a relative error of at most 0.00085.
Values may be sent and summed in bfloat16 or wider, within the bound.
No kernel may reach another device: no remote copies, remote signals or barrier semaphores. Data moves between devices by JAX's collectives and lax.ppermute only.
A program may use at most 64 MiB of HBM per device.

```python
import math
import jax
import jax.numpy as jnp
from jax import lax

D = 512
STEPS = 2
FRAG = 512
TOKENS = 4096
N_REP = 4
N_SHARD = 8


def clipped_scale():
    return 0.02 / math.sqrt(2.0 * FRAG * D)


def draw_first_moment(key, part):
    dims = (N_REP, 2, FRAG, D)
    spread = 0.15 * clipped_scale()
    return spread * jax.random.truncated_normal(key, -4.0, 4.0, dims, jnp.float32)


def draw_second_moment(key, part):
    dims = (N_REP, 2, FRAG, D)
    square = clipped_scale() * clipped_scale()
    lowest = math.log(0.01)
    highest = math.log(0.1)
    return square * jnp.exp(jax.random.uniform(key, dims, jnp.float32, lowest, highest))


def draw_targets(key, part):
    dims = (N_REP, STEPS, TOKENS, 2, FRAG)
    position = jnp.arange(FRAG, dtype=jnp.float32) / max(FRAG - 1, 1)
    growth = 0.5 * jnp.exp(math.log(8.0) * position)
    return (growth * jax.random.truncated_normal(key, -4.0, 4.0, dims, jnp.float32)).astype(jnp.bfloat16)


def levels(key, shape, shards, smallest, top_value):
    factor_of, own = 1.0, jax.random.fold_in(key, 6)
    for axis_at, blocks in shards:
        steps = jnp.exp(jax.random.uniform(jax.random.fold_in(own, axis_at), (blocks,), jnp.float32, smallest / len(shards), top_value / len(shards)))
        factor_of = factor_of * jnp.repeat(steps, shape[axis_at] // blocks).reshape([-1 if axis == axis_at else 1 for axis in range(len(shape))])
    return factor_of


def normal_values(stream_key, shape, scale, reach, split=(), held_as=jnp.bfloat16):
    factor_of = levels(stream_key, shape, split, -0.22, 0.18) if split else 1.0
    values = jax.random.normal(stream_key, shape, jnp.float32) * scale * factor_of
    return jnp.minimum(jnp.maximum(values, -reach), reach).astype(held_as)


def setup_inputs(seed: int = 0) -> dict:
    keys = jax.random.split(jax.random.key(seed), 10)
    return {
        "inner_weights": normal_values(keys[0], (N_REP, 2, FRAG, D), 1.0, 6.0, ((0, 4), (2, 8)), jnp.float32),
        "first_moment": draw_first_moment(jax.random.fold_in(keys[9], 71), 0),
        "second_moment": draw_second_moment(jax.random.fold_in(keys[9], 71), 0),
        "outer_weights": normal_values(keys[3], (2, FRAG, D), 1.0, 6.0, ((1, 8),), jnp.float32),
        "outer_velocity": normal_values(keys[4], (2, FRAG, D), 0.5, 3.0, ((1, 8),), jnp.float32),
        "tokens": normal_values(keys[5], (N_REP, STEPS, TOKENS, D), 1.0, 6.0, ((0, 4), (2, 8))),
        "targets": draw_targets(jax.random.fold_in(keys[9], 71), 0),
        "step_count": jax.random.randint(keys[7], (1,), 10, 40).astype(jnp.int32),
        "first_fragment": jax.random.randint(keys[8], (1,), 0, 2).astype(jnp.int32),
    }


beta_one = 0.9
beta_two = 0.95
inner_rate = 0.1
adam_eps = 1e-08
decay_rate = 0.1
clip_norm = 0.02
outer_rate = 0.7
outer_momentum = 0.9
mixing = 0.5

def replica_step(weights, moment_one, moment_two, batch, target, count):
    rows = weights.shape[0] * weights.shape[1]
    width = weights.shape[2]
    flat = weights.astype(jnp.bfloat16).reshape(rows, width)
    scale = 1.0 / math.sqrt(width)
    grad_scale = scale / batch.shape[0]
    tok_dev = batch.shape[0] // N_SHARD

    def block(index, total):
        start = (index * tok_dev).astype(jnp.int32)
        piece = lax.dynamic_slice_in_dim(batch, start, tok_dev, 0)
        goal = lax.dynamic_slice_in_dim(target, start, tok_dev, 0).reshape(tok_dev, rows)
        raw = jnp.dot(piece, flat.T, preferred_element_type=jnp.float32) * scale
        residual = (raw - goal.astype(jnp.float32)).astype(jnp.bfloat16)
        term = (jnp.dot(residual.T, piece, preferred_element_type=jnp.float32) * grad_scale).astype(jnp.bfloat16)
        term = lax.optimization_barrier(term)
        return total + term.astype(jnp.float32)
    grad = lax.fori_loop(0, N_SHARD, block, jnp.zeros((rows, width), jnp.float32)).reshape(weights.shape)
    norm = jnp.sqrt(jnp.sum(grad * grad))
    clipped = grad * jnp.minimum(1.0, clip_norm / (norm + 1e-06))
    moment_one = beta_one * moment_one + (1.0 - beta_one) * clipped
    moment_two = beta_two * moment_two + (1.0 - beta_two) * clipped * clipped
    correct_one = 1.0 - jnp.power(beta_one, count)
    correct_two = 1.0 - jnp.power(beta_two, count)
    update = moment_one / correct_one / (jnp.sqrt(moment_two / correct_two) + adam_eps)
    weights = weights - inner_rate * (update + decay_rate * weights)
    return (weights, moment_one, moment_two)

def reference(inner_weights, first_moment, second_moment, outer_weights, outer_velocity, tokens, targets, step_count, first_fragment):
    first = first_fragment[0]
    inner, moment_one, moment_two = (inner_weights, first_moment, second_moment)
    outer, velocity = (outer_weights, outer_velocity)
    for step in range(STEPS):
        frag = first if step == 0 else 1 - first
        theta = lax.dynamic_index_in_dim(outer, frag, 0, keepdims=False)
        speed = lax.dynamic_index_in_dim(velocity, frag, 0, keepdims=False)
        own = lax.dynamic_index_in_dim(inner, frag, 1, keepdims=False)
        delta = lax.optimization_barrier(jnp.sum(theta[None] - own, 0)) / N_REP
        speed = outer_momentum * speed + delta
        theta = theta - outer_rate * (outer_momentum * speed + delta)
        outer = lax.dynamic_update_index_in_dim(outer, theta, frag, 0)
        velocity = lax.dynamic_update_index_in_dim(velocity, speed, frag, 0)
        count = step_count[0].astype(jnp.float32) + step

        def one_replica(items):
            return replica_step(items[0], items[1], items[2], items[3], items[4], count)
        inner, moment_one, moment_two = lax.map(one_replica, (inner, moment_one, moment_two, tokens[:, step], targets[:, step]))
        local = lax.dynamic_index_in_dim(inner, frag, 1, keepdims=False)
        merged = mixing * theta[None] + (1.0 - mixing) * local
        inner = lax.dynamic_update_index_in_dim(inner, merged, frag, 1)
    return (outer, inner)
```

```python
import functools
import math

import jax
import jax.numpy as jnp
from jax import lax
from jax.experimental import pallas as pl
from jax.experimental.pallas import tpu as pltpu
from jax.sharding import PartitionSpec as P

beta_one = 0.9
beta_two = 0.95
inner_rate = 0.1
adam_eps = 1e-08
decay_rate = 0.1
clip_norm = 0.02
outer_rate = 0.7
outer_momentum = 0.9
mixing = 0.5

F32 = jnp.float32
BF16 = jnp.bfloat16


def tree_sum(items):
    items = list(items)
    while len(items) > 1:
        items = [a + b for a, b in zip(items[0::2], items[1::2])]
    return items[0]


def nt(a, b):
    return lax.dot_general(a, b, (((1,), (1,)), ((), ())), preferred_element_type=F32)


def tn(a, b):
    return lax.dot_general(a, b, (((0,), (0,)), ((), ())), preferred_element_type=F32)


def chunk_kernel(scale, grad_scale, at_ref, w_ref, xo_ref, xs_ref, to_ref, ts_ref, out_ref):
    w = w_ref[...]
    total = None
    for x_ref, t_ref in ((xo_ref, to_ref), (xs_ref, ts_ref)):
        x = x_ref[...]
        res = (nt(x, w) * scale - t_ref[...].astype(F32)).astype(BF16)
        term = tn(res, x)
        total = term if total is None else total + term
    out_ref[...] = (total * grad_scale).astype(BF16)


def chunk_grad(scale, grad_scale, at, w, own_x, sib_x, own_t, sib_t):
    rows, width = w.shape
    toks = own_x.shape[0]
    full = lambda i, at: (0, 0)
    pick = lambda i, at: (at[0], 0, 0)
    return pl.pallas_call(
        functools.partial(chunk_kernel, scale, grad_scale),
        grid_spec=pltpu.PrefetchScalarGridSpec(
            num_scalar_prefetch=1,
            grid=(1,),
            in_specs=[
                pl.BlockSpec((rows, width), full),
                pl.BlockSpec((toks, width), full),
                pl.BlockSpec((toks, width), full),
                pl.BlockSpec((None, toks, rows), pick),
                pl.BlockSpec((None, toks, rows), pick),
            ],
            out_specs=pl.BlockSpec((rows, width), full),
        ),
        out_shape=jax.ShapeDtypeStruct((rows, width), BF16),
        cost_estimate=pl.CostEstimate(
            flops=8 * rows * toks * width, bytes_accessed=6 * toks * width, transcendentals=0
        ),
        name="chunk_grad",
    )(at, w, own_x, sib_x, own_t, sib_t)


def gram_kernel(at_ref, ho_ref, hs_ref, xo_ref, xs_ref, out_ref):
    out_ref[...] = (tn(ho_ref[...], xo_ref[...]) + tn(hs_ref[...], xs_ref[...])).astype(BF16)


def gram(at, own_x, sib_x):
    toks, width = own_x.shape
    full = lambda i, at: (0, 0)
    half = lambda i, at: (0, at[0])
    return pl.pallas_call(
        gram_kernel,
        grid_spec=pltpu.PrefetchScalarGridSpec(
            num_scalar_prefetch=1,
            grid=(1,),
            in_specs=[
                pl.BlockSpec((toks, width // 2), half),
                pl.BlockSpec((toks, width // 2), half),
                pl.BlockSpec((toks, width), full),
                pl.BlockSpec((toks, width), full),
            ],
            out_specs=pl.BlockSpec((width // 2, width), full),
        ),
        out_shape=jax.ShapeDtypeStruct((width // 2, width), BF16),
        cost_estimate=pl.CostEstimate(
            flops=2 * toks * width * width, bytes_accessed=4 * toks * width, transcendentals=0
        ),
        name="gram",
    )(at, own_x, sib_x, own_x, sib_x)


def fold(x):
    rows, width = x.shape
    tiles = [x[i : i + 8] for i in range(0, rows, 8)]
    while len(tiles) > 1:
        tiles = [a + b for a, b in zip(tiles[0::2], tiles[1::2])]
    x = tiles[0]
    lanes = [x[:, i : i + 128] for i in range(0, width, 128)]
    return functools.reduce(lambda a, b: a + b, lanes)


def sum_kernel(*refs):
    grad_ref, squares_ref = refs[-2:]
    grad = tree_sum(ref[...].astype(F32) for ref in refs[:-2])
    grad_ref[...] = grad
    squares_ref[...] = fold(grad * grad)


def sum_pieces(pieces):
    rows, width = pieces[0].shape
    return pl.pallas_call(
        sum_kernel,
        out_shape=[
            jax.ShapeDtypeStruct((rows, width), F32),
            jax.ShapeDtypeStruct((8, 128), F32),
        ],
        name="sum_pieces",
    )(*pieces)


def correct_kernel(count, factor, place_ref, *refs):
    grad_ref, squares_ref = refs[-2:]
    dw_ref, go_ref, gs_ref = refs[count : count + 3]
    half = go_ref.shape[0]
    total = tree_sum(ref[...].astype(F32) for ref in refs[:count])
    p = place_ref[0]
    extra = None
    for at, g_ref in ((p, go_ref), (1 - p, gs_ref)):
        dw = dw_ref[:, pl.ds(pl.multiple_of(at * half, half), half)]
        high = dw.astype(BF16)
        low = (dw - high.astype(F32)).astype(BF16)
        g = g_ref[...]
        term = jnp.dot(high, g, preferred_element_type=F32) + jnp.dot(
            low, g, preferred_element_type=F32
        )
        extra = term if extra is None else extra + term
    grad = total + factor * extra
    grad_ref[...] = grad
    squares_ref[...] = fold(grad * grad)


def corrected(factor, place, pieces, dw, own_g, sib_g):
    rows, width = dw.shape
    vmem = pl.BlockSpec(memory_space=pltpu.VMEM)
    return pl.pallas_call(
        functools.partial(correct_kernel, len(pieces), factor),
        in_specs=[pl.BlockSpec(memory_space=pltpu.SMEM)] + [vmem] * (len(pieces) + 3),
        out_specs=[vmem, vmem],
        out_shape=[
            jax.ShapeDtypeStruct((rows, width), F32),
            jax.ShapeDtypeStruct((8, 128), F32),
        ],
        name="corrected",
    )(place, *pieces, dw, own_g, sib_g)


def adam(grad, norm_refs, one, two, moment_one, moment_two, weights):
    squares = jnp.sum(tree_sum(ref[...] for ref in norm_refs))
    norm = jnp.sqrt(jnp.full((1, 1), squares, F32))
    clipped = grad * jnp.minimum(1.0, clip_norm / (norm + 1e-06))
    moment_one = beta_one * moment_one + (1.0 - beta_one) * clipped
    moment_two = beta_two * moment_two + (1.0 - beta_two) * clipped * clipped
    update = moment_one / one / (jnp.sqrt(moment_two / two) + adam_eps)
    return moment_one, moment_two, update, weights - inner_rate * (update + decay_rate * weights)


def outer_step(theta, speed, delta):
    speed = outer_momentum * speed + delta
    return theta - outer_rate * (outer_momentum * speed + delta)


def first_kernel(
    replicas, count, first_ref, correct_ref, grad_ref, m_ref, v_ref, w_ref, outer_ref, vel_ref, *refs
):
    sums = refs[:replicas]
    norms = refs[replicas : replicas + count]
    m_out, v_out, w_out, dw_out, theta_out, total_out, send_out = refs[replicas + count :]
    rows = grad_ref.shape[0] // 2
    first = first_ref[0]
    sends = []
    for frag in range(2):
        part = pl.ds(frag * rows, rows)
        m, v, update, after = adam(
            grad_ref[part, :], norms, correct_ref[0], correct_ref[1], m_ref[frag], v_ref[frag], w_ref[frag]
        )
        m_out[frag] = m
        v_out[frag] = v
        sends.append(update)
        total = tree_sum(ref[frag] for ref in sums)
        total_out[frag] = total
        old = outer_ref[frag]
        theta = outer_step(old, vel_ref[frag], old - total * (1.0 / replicas))
        now = first == frag
        theta_out[frag] = jnp.where(now, theta, old)
        after = jnp.where(now, mixing * theta + (1.0 - mixing) * after, after)
        w_out[frag] = after
        dw_out[part, :] = after.astype(BF16).astype(F32) - w_ref[frag].astype(BF16).astype(F32)
    send_out[...] = jnp.where(first == 0, sends[1], sends[0]).astype(BF16)


def last_kernel(
    replicas, count, first_ref, correct_ref, grad_ref, m_ref, v_ref, w_ref, outer_ref, vel_ref, total_ref, *refs
):
    updates = refs[:replicas]
    norms = refs[replicas : replicas + count]
    outer_out, inner_out = refs[replicas + count :]
    rows = grad_ref.shape[0] // 2
    first = first_ref[0]
    moved = tree_sum(ref[...].astype(F32) for ref in updates)
    for frag in range(2):
        part = pl.ds(frag * rows, rows)
        after = adam(
            grad_ref[part, :], norms, correct_ref[2], correct_ref[3], m_ref[frag], v_ref[frag], w_ref[frag]
        )[3]
        old = outer_ref[frag]
        mean = ((1.0 - inner_rate * decay_rate) * total_ref[frag] - inner_rate * moved) * (1.0 / replicas)
        theta = outer_step(old, vel_ref[frag], old - mean)
        now = first != frag
        outer_out[frag] = jnp.where(now, theta, old)
        inner_out[frag] = jnp.where(now, mixing * theta + (1.0 - mixing) * after, after)


def body(
    inner_weights,
    first_moment,
    second_moment,
    outer_weights,
    outer_velocity,
    tokens,
    targets,
    step_count,
    first_fragment,
):
    weights = inner_weights[0]
    rows, width = weights.shape[1:]
    replicas = lax.axis_size("rep")
    shards = lax.axis_size("shard")
    chips = shards // 2
    toks = tokens.shape[2]
    scale = 1.0 / math.sqrt(width)
    grad_scale = scale / (toks * shards)
    index = lax.axis_index("shard")
    core = index % 2
    chip = index // 2

    def swap(x, axis, size, by):
        return lax.ppermute(x, axis, [(i, i ^ by) for i in range(size)])

    sibling = lambda x: swap(x, "shard", shards, 1)
    across = lambda x, by: swap(x, "shard", shards, 2 * by)
    over_rep = lambda x, by: x if by == 0 else swap(x, "rep", replicas, by)

    lowered = weights.astype(BF16).reshape(2 * rows, width)
    held = [lowered] + [across(lowered, k) for k in range(1, chips)]

    own_x = [tokens[0, s] for s in range(2)]
    sib_x = [sibling(x) for x in own_x]

    own_t, sib_t = [], []
    for s in range(2):
        goal = targets[0, s].reshape(toks, 2, chips, 2, rows)
        arrange = lambda y: y.transpose(2, 0, 1, 3).reshape(chips, toks, 2 * rows)
        own_t.append(arrange(lax.dynamic_index_in_dim(goal, core, 3, keepdims=False)))
        sib_t.append(sibling(arrange(lax.dynamic_index_in_dim(goal, 1 - core, 3, keepdims=False))))

    place = [jnp.reshape(chip ^ k, (1,)).astype(jnp.int32) for k in range(chips)]
    side = jnp.reshape(core, (1,)).astype(jnp.int32)

    def pieces(s):
        made = [
            chunk_grad(scale, grad_scale, place[k], held[k], own_x[s], sib_x[s], own_t[s], sib_t[s])
            for k in range(chips)
        ]
        return [made[0]] + [across(made[k], k) for k in range(1, chips)]

    def norm_parts(squares):
        both = squares + sibling(squares)
        return [both] + [across(both, k) for k in range(1, chips)]

    sums = [over_rep(weights, k) for k in range(replicas)]

    grad, squares = sum_pieces(pieces(0))
    norms = norm_parts(squares)

    half = gram(side, own_x[1], sib_x[1]).reshape(chips, width // shards, width)
    strips = [lax.dynamic_index_in_dim(half, chip ^ k, 0, keepdims=False) for k in range(chips)]
    strip = tree_sum(
        x.astype(F32) for x in [strips[0]] + [across(strips[k], k) for k in range(1, chips)]
    ).astype(BF16)
    own_g = jnp.zeros((chips, width // shards, width), BF16)
    for k in range(chips):
        own_g = lax.dynamic_update_index_in_dim(
            own_g, strip if k == 0 else across(strip, k), chip ^ k, 0
        )
    own_g = own_g.reshape(width // 2, width)
    sib_g = sibling(own_g)

    count = step_count[0].astype(F32)
    correct = jnp.stack(
        [1.0 - jnp.power(beta, count + s) for s in range(2) for beta in (beta_one, beta_two)]
    )
    smem = pl.BlockSpec(memory_space=pltpu.SMEM)
    vmem = pl.BlockSpec(memory_space=pltpu.VMEM)
    state = jax.ShapeDtypeStruct((2, rows, width), F32)
    flat = jax.ShapeDtypeStruct((2 * rows, width), F32)
    m, v, middle, change, outer, total, moved = pl.pallas_call(
        functools.partial(first_kernel, replicas, chips),
        in_specs=[smem, smem] + [vmem] * (6 + replicas + chips),
        out_specs=[vmem] * 7,
        out_shape=[state, state, state, flat, state, state, jax.ShapeDtypeStruct((rows, width), BF16)],
        name="first_update",
    )(
        first_fragment,
        correct,
        grad,
        first_moment[0],
        second_moment[0],
        weights,
        outer_weights,
        outer_velocity,
        *sums,
        *norms,
    )
    updates = [over_rep(moved, k) for k in range(replicas)]

    grad, squares = corrected(scale * grad_scale, side, pieces(1), change, own_g, sib_g)
    norms = norm_parts(squares)
    new_outer, new_inner = pl.pallas_call(
        functools.partial(last_kernel, replicas, chips),
        in_specs=[smem, smem] + [vmem] * (7 + replicas + chips),
        out_specs=[vmem] * 2,
        out_shape=[state, state],
        name="last_update",
    )(first_fragment, correct, grad, m, v, middle, outer, outer_velocity, total, *updates, *norms)
    return (new_outer, new_inner[None])


def solution(mesh):
    in_specs = (
        P("rep", None, "shard", None),
        P("rep", None, "shard", None),
        P("rep", None, "shard", None),
        P(None, "shard", None),
        P(None, "shard", None),
        P("rep", None, "shard", None),
        P("rep", None, "shard", None, None),
        P(),
        P(),
    )
    out_specs = (P(None, "shard", None), P("rep", None, "shard", None))
    return jax.shard_map(body, mesh=mesh, in_specs=in_specs, out_specs=out_specs, check_vma=False)
```

```python
import functools
import math

import jax
import jax.numpy as jnp
from jax import lax
from jax.experimental import pallas as pl
from jax.experimental.pallas import tpu as pltpu
from jax.sharding import PartitionSpec as P

beta_one = 0.9
beta_two = 0.95
inner_rate = 0.1
adam_eps = 1e-08
decay_rate = 0.1
clip_norm = 0.02
outer_rate = 0.7
outer_momentum = 0.9
mixing = 0.5

F32 = jnp.float32
BF16 = jnp.bfloat16
VMEM_BYTES = 16 * 1024 * 1024


def tree_sum(items):
    items = list(items)
    while len(items) > 1:
        items = [a + b for a, b in zip(items[0::2], items[1::2])]
    return items[0]


def nt(a, b):
    return lax.dot_general(a, b, (((1,), (1,)), ((), ())), preferred_element_type=F32)


def tn(a, b):
    return lax.dot_general(a, b, (((0,), (0,)), ((), ())), preferred_element_type=F32)


def call(kernel, out_shape, scalars, arrays, name, after=(), flops=0):
    vmem = pl.BlockSpec(memory_space=pltpu.VMEM)

    def run(*refs):
        count = len(scalars) + len(arrays)
        kernel(*refs[:count], *refs[count + len(after) :])

    return pl.pallas_call(
        run,
        in_specs=[pl.BlockSpec(memory_space=pltpu.SMEM)] * len(scalars)
        + [vmem] * len(arrays)
        + [pl.BlockSpec(memory_space=pl.ANY)] * len(after),
        out_specs=[vmem] * len(out_shape),
        out_shape=out_shape,
        compiler_params=pltpu.CompilerParams(vmem_limit_bytes=VMEM_BYTES),
        cost_estimate=pl.CostEstimate(flops=flops, bytes_accessed=1024, transcendentals=0),
        name=name,
    )(*scalars, *arrays, *after)


def lower_kernel(w_ref, out_ref):
    rows = w_ref.shape[1]
    for frag in range(2):
        out_ref[pl.ds(frag * rows, rows), :] = w_ref[frag].astype(BF16)


def split_kernel(rows, side_ref, goal_ref, keep_ref, send_ref):
    core = side_ref[0]
    first, second = (goal_ref[:, frag, :].astype(F32) for frag in range(2))
    for chip in range(keep_ref.shape[0]):
        parts = []
        for which in range(2):
            at = (2 * chip + which) * rows
            parts.append(
                jnp.concatenate([first[:, at : at + rows], second[:, at : at + rows]], 1).astype(BF16)
            )

        @pl.when(core == 0)
        def _():
            keep_ref[chip] = parts[0]
            send_ref[chip] = parts[1]

        @pl.when(core != 0)
        def _():
            keep_ref[chip] = parts[1]
            send_ref[chip] = parts[0]


def chunk_kernel(scale, grad_scale, group, place_ref, *refs):
    size = len(group)
    w_refs = refs[:size]
    xo_ref, xs_ref, to_ref, ts_ref = refs[size : size + 4]
    outs = refs[size + 4 :]
    rows = w_refs[0].shape[0]
    w = jnp.concatenate([ref[...] for ref in w_refs], 0)
    total = None
    for x_ref, t_ref in ((xo_ref, to_ref), (xs_ref, ts_ref)):
        x = x_ref[...]
        goal = jnp.concatenate([t_ref[place_ref[k]] for k in group], 1)
        res = (nt(x, w) * scale - goal.astype(F32)).astype(BF16)
        term = tn(res, x)
        total = term if total is None else total + term
    total = (total * grad_scale).astype(BF16)
    for i, ref in enumerate(outs):
        ref[...] = total[i * rows : (i + 1) * rows]


def gram_kernel(side_ref, place_ref, xo_ref, xs_ref, *refs):
    outs, scratch = refs[:-1], refs[-1]
    rows, width = outs[0].shape
    part = pl.ds(pl.multiple_of(side_ref[0] * (width // 2), width // 2), width // 2)
    scratch[...] = (tn(xo_ref[:, part], xo_ref[...]) + tn(xs_ref[:, part], xs_ref[...])).astype(BF16)
    for k, ref in enumerate(outs):
        ref[...] = scratch[pl.ds(pl.multiple_of(place_ref[k] * rows, rows), rows), :]


def gather_kernel(place_ref, *refs):
    strips, out_ref = refs[:-1], refs[-1]
    rows = strips[0].shape[0]
    for k, ref in enumerate(strips):
        out_ref[pl.ds(pl.multiple_of(place_ref[k] * rows, rows), rows), :] = ref[...]


def add_kernel(*refs):
    refs[-1][...] = tree_sum(ref[...].astype(F32) for ref in refs[:-1]).astype(refs[-1].dtype)


def fold(x):
    rows, width = x.shape
    tiles = [x[i : i + 8] for i in range(0, rows, 8)]
    while len(tiles) > 1:
        tiles = [a + b for a, b in zip(tiles[0::2], tiles[1::2])]
    x = tiles[0]
    lanes = [x[:, i : i + 128] for i in range(0, width, 128)]
    return functools.reduce(lambda a, b: a + b, lanes)


def sum_kernel(*refs):
    grad_ref, squares_ref = refs[-2:]
    grad = tree_sum(ref[...].astype(F32) for ref in refs[:-2])
    grad_ref[...] = grad
    squares_ref[...] = fold(grad * grad)


def correct_kernel(count, factor, side_ref, *refs):
    grad_ref, squares_ref = refs[-2:]
    dw_ref, go_ref, gs_ref = refs[count : count + 3]
    half = go_ref.shape[0]
    total = tree_sum(ref[...].astype(F32) for ref in refs[:count])
    p = side_ref[0]
    extra = None
    for at, g_ref in ((p, go_ref), (1 - p, gs_ref)):
        dw = dw_ref[:, pl.ds(pl.multiple_of(at * half, half), half)]
        high = dw.astype(BF16)
        low = (dw - high.astype(F32)).astype(BF16)
        g = g_ref[...]
        term = jnp.dot(high, g, preferred_element_type=F32) + jnp.dot(
            low, g, preferred_element_type=F32
        )
        extra = term if extra is None else extra + term
    grad = total + factor * extra
    grad_ref[...] = grad
    squares_ref[...] = fold(grad * grad)


def adam(grad, norm_refs, one, two, moment_one, moment_two, weights):
    squares = jnp.sum(tree_sum(ref[...] for ref in norm_refs))
    norm = jnp.sqrt(jnp.full((1, 1), squares, F32))
    clipped = grad * jnp.minimum(1.0, clip_norm / (norm + 1e-06))
    moment_one = beta_one * moment_one + (1.0 - beta_one) * clipped
    moment_two = beta_two * moment_two + (1.0 - beta_two) * clipped * clipped
    update = moment_one / one / (jnp.sqrt(moment_two / two) + adam_eps)
    return moment_one, moment_two, update, weights - inner_rate * (update + decay_rate * weights)


def outer_step(theta, speed, delta):
    speed = outer_momentum * speed + delta
    return theta - outer_rate * (outer_momentum * speed + delta)


def first_kernel(
    replicas, count, first_ref, correct_ref, grad_ref, m_ref, v_ref, w_ref, outer_ref, vel_ref, *refs
):
    sums = refs[:replicas]
    norms = refs[replicas : replicas + count]
    m_out, v_out, w_out, dw_out, theta_out, total_out, send_out = refs[replicas + count :]
    rows = grad_ref.shape[0] // 2
    first = first_ref[0]
    sends = []
    for frag in range(2):
        part = pl.ds(frag * rows, rows)
        m, v, update, after = adam(
            grad_ref[part, :], norms, correct_ref[0], correct_ref[1], m_ref[frag], v_ref[frag], w_ref[frag]
        )
        m_out[frag] = m
        v_out[frag] = v
        sends.append(update)
        total = tree_sum(ref[frag] for ref in sums)
        total_out[frag] = total
        old = outer_ref[frag]
        theta = outer_step(old, vel_ref[frag], old - total * (1.0 / replicas))
        now = first == frag
        theta_out[frag] = jnp.where(now, theta, old)
        after = jnp.where(now, mixing * theta + (1.0 - mixing) * after, after)
        w_out[frag] = after
        dw_out[part, :] = after.astype(BF16).astype(F32) - w_ref[frag].astype(BF16).astype(F32)
    send_out[...] = jnp.where(first == 0, sends[1], sends[0]).astype(BF16)


def last_kernel(
    replicas, count, first_ref, correct_ref, grad_ref, m_ref, v_ref, w_ref, outer_ref, vel_ref, total_ref, *refs
):
    updates = refs[:replicas]
    norms = refs[replicas : replicas + count]
    outer_out, inner_out = refs[replicas + count :]
    rows = grad_ref.shape[0] // 2
    first = first_ref[0]
    moved = tree_sum(ref[...].astype(F32) for ref in updates)
    for frag in range(2):
        part = pl.ds(frag * rows, rows)
        after = adam(
            grad_ref[part, :], norms, correct_ref[2], correct_ref[3], m_ref[frag], v_ref[frag], w_ref[frag]
        )[3]
        old = outer_ref[frag]
        mean = ((1.0 - inner_rate * decay_rate) * total_ref[frag] - inner_rate * moved) * (1.0 / replicas)
        theta = outer_step(old, vel_ref[frag], old - mean)
        now = first != frag
        outer_out[frag] = jnp.where(now, theta, old)
        inner_out[frag] = jnp.where(now, mixing * theta + (1.0 - mixing) * after, after)


def body(
    inner_weights,
    first_moment,
    second_moment,
    outer_weights,
    outer_velocity,
    tokens,
    targets,
    step_count,
    first_fragment,
):
    weights = inner_weights[0]
    rows, width = weights.shape[1:]
    replicas = lax.axis_size("rep")
    shards = lax.axis_size("shard")
    chips = shards // 2
    toks = tokens.shape[2]
    scale = 1.0 / math.sqrt(width)
    grad_scale = scale / (toks * shards)
    index = lax.axis_index("shard")
    core = index % 2
    chip = index // 2

    def swap(x, axis, size, by):
        return lax.ppermute(x, axis, [(i, i ^ by) for i in range(size)])

    sibling = lambda x: swap(x, "shard", shards, 1)
    across = lambda x, by: swap(x, "shard", shards, 2 * by)
    over_rep = lambda x, by: x if by == 0 else swap(x, "rep", replicas, by)

    shape = jax.ShapeDtypeStruct
    block = shape((2 * rows, width), BF16)
    strip_shape = shape((width // shards, width), BF16)
    tile = shape((8, 128), F32)
    state = shape((2, rows, width), F32)
    flat = shape((2 * rows, width), F32)
    side = jnp.reshape(core, (1,)).astype(jnp.int32)
    place = jnp.stack([chip ^ k for k in range(chips)]).astype(jnp.int32)

    (lowered,) = call(lower_kernel, [block], [], [weights], "lower")
    held = [lowered] + [across(lowered, k) for k in range(1, chips)]

    own_x = [tokens[0, s] for s in range(2)]
    sib_x = [sibling(x) for x in own_x]

    def split(s, after):
        out = shape((chips, toks, 2 * rows), BF16)
        return pl.pallas_call(
            lambda side_ref, goal_ref, after_ref, *outs: split_kernel(rows, side_ref, goal_ref, *outs),
            grid_spec=pltpu.PrefetchScalarGridSpec(
                num_scalar_prefetch=1,
                grid=(1,),
                in_specs=[
                    pl.BlockSpec((None, None, toks, 2, width), lambda i, side: (0, s, 0, 0, 0)),
                    pl.BlockSpec(memory_space=pl.ANY),
                ],
                out_specs=[pl.BlockSpec(out.shape, lambda i, side: (0, 0, 0))] * 2,
            ),
            out_shape=[out, out],
            compiler_params=pltpu.CompilerParams(vmem_limit_bytes=VMEM_BYTES),
            cost_estimate=pl.CostEstimate(flops=0, bytes_accessed=1024, transcendentals=0),
            name="split",
        )(side, targets, after)

    own_t, sib_t = [], []
    after = lowered
    for s in range(2):
        keep, send = split(s, after)
        own_t.append(keep)
        sib_t.append(sibling(send))
        after = keep

    def chunk_grad(s, group, after):
        return call(
            functools.partial(chunk_kernel, scale, grad_scale, group),
            [block] * len(group),
            [place],
            [held[k] for k in group] + [own_x[s], sib_x[s], own_t[s], sib_t[s]],
            "chunk_grad",
            after,
        )

    def spread(made):
        return [made[0]] + [across(made[k], k) for k in range(1, chips)]

    def norm_parts(squares):
        both = squares + sibling(squares)
        return [both] + [across(both, k) for k in range(1, chips)]

    near = list(range(max(1, chips // 2)))
    far = list(range(max(1, chips // 2), chips))
    made = chunk_grad(0, near, [])
    made = made + chunk_grad(0, far, [made[0]])
    pieces_one = spread(made)
    strips = pl.pallas_call(
        lambda side_ref, place_ref, xo, xs, after_ref, *refs: gram_kernel(side_ref, place_ref, xo, xs, *refs),
        in_specs=[pl.BlockSpec(memory_space=pltpu.SMEM)] * 2
        + [pl.BlockSpec(memory_space=pltpu.VMEM)] * 2
        + [pl.BlockSpec(memory_space=pl.ANY)],
        out_specs=[pl.BlockSpec(memory_space=pltpu.VMEM)] * chips,
        out_shape=[strip_shape] * chips,
        scratch_shapes=[pltpu.VMEM((width // 2, width), BF16)],
        compiler_params=pltpu.CompilerParams(vmem_limit_bytes=VMEM_BYTES),
        cost_estimate=pl.CostEstimate(flops=0, bytes_accessed=1024, transcendentals=0),
        name="gram",
    )(side, place, own_x[1], sib_x[1], made[-1])
    strips = spread(strips)
    made = chunk_grad(1, near + far, [strips[0]])
    pieces_two = spread(made)

    sums = [over_rep(weights, k) for k in range(replicas)]

    grad, squares = call(sum_kernel, [flat, tile], [], pieces_one, "sum_pieces")
    norms = norm_parts(squares)

    (strip,) = call(add_kernel, [strip_shape], [], strips, "strip")
    (own_g,) = call(
        gather_kernel,
        [shape((width // 2, width), BF16)],
        [place],
        [strip] + [across(strip, k) for k in range(1, chips)],
        "gather_strips",
    )
    sib_g = sibling(own_g)

    count = step_count[0].astype(F32)
    correct = jnp.stack(
        [1.0 - jnp.power(beta, count + s) for s in range(2) for beta in (beta_one, beta_two)]
    )
    m, v, middle, change, outer, total, moved = call(
        functools.partial(first_kernel, replicas, chips),
        [state, state, state, flat, state, state, shape((rows, width), BF16)],
        [first_fragment, correct],
        [grad, first_moment[0], second_moment[0], weights, outer_weights, outer_velocity, *sums, *norms],
        "first_update",
    )
    updates = [over_rep(moved, k) for k in range(replicas)]

    grad, squares = call(
        functools.partial(correct_kernel, chips, scale * grad_scale),
        [flat, tile],
        [side],
        [*pieces_two, change, own_g, sib_g],
        "corrected",
    )
    norms = norm_parts(squares)
    new_outer, new_inner = call(
        functools.partial(last_kernel, replicas, chips),
        [state, state],
        [first_fragment, correct],
        [grad, m, v, middle, outer, outer_velocity, total, *updates, *norms],
        "last_update",
    )
    return (new_outer, new_inner[None])


def solution(mesh):
    in_specs = (
        P("rep", None, "shard", None),
        P("rep", None, "shard", None),
        P("rep", None, "shard", None),
        P(None, "shard", None),
        P(None, "shard", None),
        P("rep", None, "shard", None),
        P("rep", None, "shard", None, None),
        P(),
        P(),
    )
    out_specs = (P(None, "shard", None), P("rep", None, "shard", None))
    return jax.shard_map(body, mesh=mesh, in_specs=in_specs, out_specs=out_specs, check_vma=False)
```

```python
import functools
import math

import jax
import jax.numpy as jnp
from jax import lax
from jax.experimental import pallas as pl
from jax.experimental.pallas import tpu as pltpu
from jax.sharding import PartitionSpec as P

beta_one = 0.9
beta_two = 0.95
inner_rate = 0.1
adam_eps = 1e-08
decay_rate = 0.1
clip_norm = 0.02
outer_rate = 0.7
outer_momentum = 0.9
mixing = 0.5

F32 = jnp.float32
BF16 = jnp.bfloat16
VMEM_BYTES = 16 * 1024 * 1024


def tree_sum(items):
    items = list(items)
    while len(items) > 1:
        items = [a + b for a, b in zip(items[0::2], items[1::2])]
    return items[0]


def nt(a, b):
    return lax.dot_general(a, b, (((1,), (1,)), ((), ())), preferred_element_type=F32)


def tn(a, b):
    return lax.dot_general(a, b, (((0,), (0,)), ((), ())), preferred_element_type=F32)


def call(kernel, out_shape, scalars, arrays, name, after=(), scratch=(), flops=0):
    vmem = pl.BlockSpec(memory_space=pltpu.VMEM)

    def run(*refs):
        count = len(scalars) + len(arrays)
        kernel(*refs[:count], *refs[count + len(after) :])

    return pl.pallas_call(
        run,
        in_specs=[pl.BlockSpec(memory_space=pltpu.SMEM)] * len(scalars)
        + [vmem] * len(arrays)
        + [pl.BlockSpec(memory_space=pl.ANY)] * len(after),
        out_specs=[vmem] * len(out_shape),
        out_shape=out_shape,
        scratch_shapes=list(scratch),
        compiler_params=pltpu.CompilerParams(vmem_limit_bytes=VMEM_BYTES),
        cost_estimate=pl.CostEstimate(flops=flops, bytes_accessed=1024, transcendentals=0),
        name=name,
    )(*scalars, *arrays, *after)


def lower_kernel(w_ref, out_ref):
    rows = w_ref.shape[1]
    for frag in range(2):
        out_ref[pl.ds(frag * rows, rows), :] = w_ref[frag].astype(BF16)


def split_kernel(rows, side_ref, own_ref, sib_ref, *outs):
    core = side_ref[0]
    for step in range(2):
        for goal_ref, out_ref in zip((own_ref, sib_ref), outs):
            first, second = (goal_ref[0, step, :, frag, :].astype(F32) for frag in range(2))
            for chip in range(out_ref.shape[1]):
                for which in range(2):

                    @pl.when(core == which)
                    def _():
                        at = (2 * chip + which) * rows
                        pair = [first[:, at : at + rows], second[:, at : at + rows]]
                        out_ref[step, chip] = jnp.concatenate(pair, 1).astype(BF16)


def chunk_grad(scale, grad_scale, step, group, place_ref, w_refs, token_refs, goal_refs):
    w = jnp.concatenate([ref[...] for ref in w_refs], 0)
    total = None
    for x_ref, t_ref in zip(token_refs, goal_refs):
        x = x_ref[step]
        goal = jnp.concatenate([t_ref[step, place_ref[k]] for k in group], 1)
        res = (nt(x, w) * scale - goal.astype(F32)).astype(BF16)
        term = tn(res, x)
        total = term if total is None else total + term
    total = (total * grad_scale).astype(BF16)
    rows = w_refs[0].shape[0]
    return [total[i * rows : (i + 1) * rows] for i in range(len(group))]


def near_kernel(scales, group, place_ref, *refs):
    size = len(group)
    w_refs, token_refs, goal_refs = refs[:size], refs[size : size + 2], refs[size + 2 : size + 4]
    outs = refs[size + 4 :]
    for step in range(2):
        made = chunk_grad(*scales, step, group, place_ref, w_refs, token_refs, goal_refs)
        for ref, value in zip(outs[step * size :], made):
            ref[...] = value


def far_kernel(scales, near, far, place_ref, *refs):
    size = len(far)
    chips = len(near) + size
    w_refs, token_refs, goal_refs = refs[:size], refs[size : size + 2], refs[size + 2 : size + 4]
    near_refs = refs[size + 4 : size + 4 + len(near)]
    strip_refs = refs[size + 4 + len(near) : size + 4 + len(near) + chips]
    weights_ref, *outs, copy_ref = refs[size + 4 + len(near) + chips :]
    made = dict(zip(near, (ref[...] for ref in near_refs)))
    made.update(zip(far, chunk_grad(*scales, 0, far, place_ref, w_refs, token_refs, goal_refs)))
    strip = tree_sum(ref[...].astype(F32) for ref in strip_refs).astype(BF16)
    for k, ref in enumerate(outs[:chips]):
        rows = made[k].shape[0]
        ref[pl.ds(0, rows), :] = made[k]
        ref[pl.ds(rows, strip.shape[0]), :] = strip
    made = chunk_grad(*scales, 1, far, place_ref, w_refs, token_refs, goal_refs)
    for ref, value in zip(outs[chips:], made):
        ref[...] = value
    copy_ref[...] = weights_ref[...]


def halve_kernel(*refs):
    count = len(refs) // 3
    for keep_ref, got_ref, out_ref in zip(refs[:count], refs[count:], refs[2 * count :]):
        out_ref[...] = (keep_ref[...].astype(F32) + got_ref[...].astype(F32)).astype(BF16)


def gram_kernel(step, side_ref, place_ref, xo_ref, xs_ref, *refs):
    outs, scratch = refs[:-1], refs[-1]
    rows, width = outs[0].shape
    part = pl.ds(pl.multiple_of(side_ref[0] * (width // 2), width // 2), width // 2)
    total = tn(xo_ref[step, :, part], xo_ref[step]) + tn(xs_ref[step, :, part], xs_ref[step])
    scratch[...] = total.astype(BF16)
    for k, ref in enumerate(outs):
        ref[...] = scratch[pl.ds(pl.multiple_of(place_ref[k] * rows, rows), rows), :]


def add_kernel(*refs):
    refs[-1][...] = tree_sum(ref[...] for ref in refs[:-1])


def sum_kernel(place_ref, *refs):
    pieces, (grad_ref, squares_ref, gram_ref) = refs[:-3], refs[-3:]
    rows = grad_ref.shape[0]
    strip = pieces[0].shape[0] - rows
    grad = tree_sum(ref[pl.ds(0, rows), :].astype(F32) for ref in pieces)
    grad_ref[...] = grad
    squares_ref[...] = fold(grad * grad)
    for k, ref in enumerate(pieces):
        gram_ref[pl.ds(pl.multiple_of(place_ref[k] * strip, strip), strip), :] = ref[pl.ds(rows, strip), :]


def fold(x):
    rows, width = x.shape
    tiles = [x[i : i + 8] for i in range(0, rows, 8)]
    while len(tiles) > 1:
        tiles = [a + b for a, b in zip(tiles[0::2], tiles[1::2])]
    x = tiles[0]
    lanes = [x[:, i : i + 128] for i in range(0, width, 128)]
    return functools.reduce(lambda a, b: a + b, lanes)


def correct_kernel(count, factor, side_ref, *refs):
    grad_ref, squares_ref = refs[-2:]
    dw_ref, go_ref, gs_ref = refs[count : count + 3]
    half = go_ref.shape[0]
    total = tree_sum(ref[...].astype(F32) for ref in refs[:count])
    p = side_ref[0]
    extra = None
    for at, g_ref in ((p, go_ref), (1 - p, gs_ref)):
        dw = dw_ref[:, pl.ds(pl.multiple_of(at * half, half), half)]
        high = dw.astype(BF16)
        low = (dw - high.astype(F32)).astype(BF16)
        g = g_ref[...]
        term = jnp.dot(high, g, preferred_element_type=F32) + jnp.dot(
            low, g, preferred_element_type=F32
        )
        extra = term if extra is None else extra + term
    grad = total + factor * extra
    grad_ref[...] = grad
    squares_ref[...] = fold(grad * grad)


def adam(grad, norm_refs, one, two, moment_one, moment_two, weights):
    squares = jnp.sum(tree_sum(ref[...] for ref in norm_refs))
    norm = jnp.sqrt(jnp.full((1, 1), squares, F32))
    clipped = grad * jnp.minimum(1.0, clip_norm / (norm + 1e-06))
    moment_one = beta_one * moment_one + (1.0 - beta_one) * clipped
    moment_two = beta_two * moment_two + (1.0 - beta_two) * clipped * clipped
    update = moment_one / one / (jnp.sqrt(moment_two / two) + adam_eps)
    return moment_one, moment_two, update, weights - inner_rate * (update + decay_rate * weights)


def outer_step(theta, speed, delta):
    speed = outer_momentum * speed + delta
    return theta - outer_rate * (outer_momentum * speed + delta)


def first_kernel(
    replicas, count, first_ref, correct_ref, grad_ref, m_ref, v_ref, w_ref, outer_ref, vel_ref, total_ref, *refs
):
    norms = refs[:count]
    m_out, v_out, w_out, dw_out, theta_out, send_out = refs[count:]
    rows = grad_ref.shape[0] // 2
    first = first_ref[0]
    sends = []
    for frag in range(2):
        part = pl.ds(frag * rows, rows)
        m, v, update, after = adam(
            grad_ref[part, :], norms, correct_ref[0], correct_ref[1], m_ref[frag], v_ref[frag], w_ref[frag]
        )
        m_out[frag] = m
        v_out[frag] = v
        sends.append(update)
        old = outer_ref[frag]
        theta = outer_step(old, vel_ref[frag], old - total_ref[frag] * (1.0 / replicas))
        now = first == frag
        theta_out[frag] = jnp.where(now, theta, old)
        after = jnp.where(now, mixing * theta + (1.0 - mixing) * after, after)
        w_out[frag] = after
        dw_out[part, :] = after.astype(BF16).astype(F32) - w_ref[frag].astype(BF16).astype(F32)
    send_out[...] = jnp.where(first == 0, sends[1], sends[0]).astype(BF16)


def last_kernel(
    replicas, count, first_ref, correct_ref, grad_ref, m_ref, v_ref, w_ref, outer_ref, vel_ref, total_ref, *refs
):
    updates = refs[:replicas]
    norms = refs[replicas : replicas + count]
    outer_out, inner_out = refs[replicas + count :]
    rows = grad_ref.shape[0] // 2
    first = first_ref[0]
    moved = tree_sum(ref[...].astype(F32) for ref in updates)
    for frag in range(2):
        part = pl.ds(frag * rows, rows)
        after = adam(
            grad_ref[part, :], norms, correct_ref[2], correct_ref[3], m_ref[frag], v_ref[frag], w_ref[frag]
        )[3]
        old = outer_ref[frag]
        mean = ((1.0 - inner_rate * decay_rate) * total_ref[frag] - inner_rate * moved) * (1.0 / replicas)
        theta = outer_step(old, vel_ref[frag], old - mean)
        now = first != frag
        outer_out[frag] = jnp.where(now, theta, old)
        inner_out[frag] = jnp.where(now, mixing * theta + (1.0 - mixing) * after, after)


def body(
    inner_weights,
    first_moment,
    second_moment,
    outer_weights,
    outer_velocity,
    tokens,
    targets,
    step_count,
    first_fragment,
):
    weights = inner_weights[0]
    rows, width = weights.shape[1:]
    replicas = lax.axis_size("rep")
    shards = lax.axis_size("shard")
    chips = shards // 2
    toks = tokens.shape[2]
    scale = 1.0 / math.sqrt(width)
    grad_scale = scale / (toks * shards)
    index = lax.axis_index("shard")
    core = index % 2
    chip = index // 2

    def swap(x, axis, size, by):
        return lax.ppermute(x, axis, [(i, i ^ by) for i in range(size)])

    sibling = lambda x: swap(x, "shard", shards, 1)
    across = lambda x, by: swap(x, "shard", shards, 2 * by)
    over_rep = lambda x, by: x if by == 0 else swap(x, "rep", replicas, by)

    shape = jax.ShapeDtypeStruct
    block = shape((2 * rows, width), BF16)
    tile = shape((8, 128), F32)
    state = shape((2, rows, width), F32)
    flat = shape((2 * rows, width), F32)
    side = jnp.reshape(core, (1,)).astype(jnp.int32)
    place = jnp.stack([chip ^ k for k in range(chips)]).astype(jnp.int32)

    (lowered,) = call(lower_kernel, [block], [], [weights], "lower")
    held = [lowered] + [across(lowered, k) for k in range(1, chips)]

    own_x = tokens[0]
    sib_x = sibling(own_x)

    swapped = sibling(targets)

    strip_shape = shape((width // shards, width), BF16)
    strips = call(
        functools.partial(gram_kernel, 1),
        [strip_shape] * chips,
        [side, place],
        [own_x, sib_x],
        "gram",
        [lowered],
        [pltpu.VMEM((width // 2, width), BF16)],
    )

    def spread(made):
        return [made[0]] + [across(made[k], k) for k in range(1, chips)]

    def norm_parts(squares, after):
        (both,) = call(add_kernel, [tile], [], [squares, sibling(squares)], "add_cores", after)
        return [both] + [across(both, k) for k in range(1, chips)]

    parts = shape((2, chips, toks, 2 * rows), BF16)
    own_t, sib_t = call(
        functools.partial(split_kernel, rows), [parts, parts], [side], [targets, swapped], "split", [strips[0]]
    )

    near = list(range(max(1, chips // 2)))
    far = list(range(max(1, chips // 2), chips))
    scales = (scale, grad_scale)
    made = call(
        functools.partial(near_kernel, scales, near),
        [block] * (2 * len(near)),
        [place],
        [held[k] for k in near] + [own_x, sib_x, own_t, sib_t],
        "near_grad",
    )
    joint = call(
        functools.partial(far_kernel, scales, near, far),
        [shape((2 * rows + width // shards, width), BF16)] * chips + [block] * len(far) + [state],
        [place],
        [held[k] for k in far] + [own_x, sib_x, own_t, sib_t, *made[: len(near)], *spread(strips), weights],
        "far_grad",
    )
    pieces_one = spread(joint[:chips])
    made = [*made[len(near) :], *joint[chips:-1]]
    early = joint[-1]
    keep, got = made[0::2], [across(x, 1) for x in made[1::2]]
    ready = got
    bit = 2
    while bit < chips:
        made = call(halve_kernel, [block] * len(keep), [], [*keep, *got], "halve")
        keep, got = made[0::2], [across(x, bit) for x in made[1::2]]
        bit *= 2
    pieces_two = [keep[0], got[0]]

    sums = early
    by = 1
    while by < replicas:
        (sums,) = call(add_kernel, [state], [], [sums, swap(sums, "rep", replicas, by)], "add_reps")
        by *= 2

    grad, squares, own_g = call(
        sum_kernel,
        [flat, tile, shape((width // 2, width), BF16)],
        [place],
        pieces_one,
        "sum_pieces",
        ready,
    )
    sib_g = sibling(own_g)
    norms = norm_parts(squares, [sib_g])

    count = step_count[0].astype(F32)
    correct = jnp.stack(
        [1.0 - jnp.power(beta, count + s) for s in range(2) for beta in (beta_one, beta_two)]
    )
    m, v, middle, change, outer, moved = call(
        functools.partial(first_kernel, replicas, chips),
        [state, state, state, flat, state, shape((rows, width), BF16)],
        [first_fragment, correct],
        [grad, first_moment[0], second_moment[0], weights, outer_weights, outer_velocity, sums, *norms],
        "first_update",
        pieces_two[1:],
    )
    updates = [over_rep(moved, k) for k in range(replicas)]

    grad, squares = call(
        functools.partial(correct_kernel, len(pieces_two), scale * grad_scale),
        [flat, tile],
        [side],
        [*pieces_two, change, own_g, sib_g],
        "corrected",
    )
    norms = norm_parts(squares, [])
    new_outer, new_inner = call(
        functools.partial(last_kernel, replicas, chips),
        [state, state],
        [first_fragment, correct],
        [grad, m, v, middle, outer, outer_velocity, sums, *updates, *norms],
        "last_update",
    )
    return (new_outer, new_inner[None])


def solution(mesh):
    in_specs = (
        P("rep", None, "shard", None),
        P("rep", None, "shard", None),
        P("rep", None, "shard", None),
        P(None, "shard", None),
        P(None, "shard", None),
        P("rep", None, "shard", None),
        P("rep", None, "shard", None, None),
        P(),
        P(),
    )
    out_specs = (P(None, "shard", None), P("rep", None, "shard", None))
    return jax.shard_map(body, mesh=mesh, in_specs=in_specs, out_specs=out_specs, check_vma=False)
```

```python
import functools
import math

import jax
import jax.numpy as jnp
from jax import lax
from jax.experimental import pallas as pl
from jax.experimental.pallas import tpu as pltpu
from jax.sharding import PartitionSpec as P

beta_one = 0.9
beta_two = 0.95
inner_rate = 0.1
adam_eps = 1e-08
decay_rate = 0.1
clip_norm = 0.02
outer_rate = 0.7
outer_momentum = 0.9
mixing = 0.5

F32 = jnp.float32
BF16 = jnp.bfloat16
VMEM_BYTES = 16 * 1024 * 1024


def tree_sum(items):
    items = list(items)
    while len(items) > 1:
        items = [a + b for a, b in zip(items[0::2], items[1::2])]
    return items[0]


def nt(a, b):
    return lax.dot_general(a, b, (((1,), (1,)), ((), ())), preferred_element_type=F32)


def tn(a, b):
    return lax.dot_general(a, b, (((0,), (0,)), ((), ())), preferred_element_type=F32)


def call(kernel, out_shape, scalars, arrays, name, after=(), scratch=(), flops=0):
    vmem = pl.BlockSpec(memory_space=pltpu.VMEM)

    def run(*refs):
        count = len(scalars) + len(arrays)
        kernel(*refs[:count], *refs[count + len(after) :])

    return pl.pallas_call(
        run,
        in_specs=[pl.BlockSpec(memory_space=pltpu.SMEM)] * len(scalars)
        + [vmem] * len(arrays)
        + [pl.BlockSpec(memory_space=pl.ANY)] * len(after),
        out_specs=[vmem] * len(out_shape),
        out_shape=out_shape,
        scratch_shapes=list(scratch),
        compiler_params=pltpu.CompilerParams(vmem_limit_bytes=VMEM_BYTES),
        cost_estimate=pl.CostEstimate(flops=flops, bytes_accessed=1024, transcendentals=0),
        name=name,
    )(*scalars, *arrays, *after)


def lower_kernel(w_ref, out_ref):
    rows = w_ref.shape[1]
    for frag in range(2):
        out_ref[pl.ds(frag * rows, rows), :] = w_ref[frag].astype(BF16)


def split_kernel(rows, side_ref, own_ref, sib_ref, *outs):
    core = side_ref[0]
    toks, width = own_ref.shape[2], own_ref.shape[4]
    size = math.gcd(toks, 256)
    row = lax.broadcasted_iota(jnp.int32, (size, 2 * size), 0)
    column = lax.broadcasted_iota(jnp.int32, (size, 2 * size), 1)
    takes = [(column == 2 * row + frag).astype(BF16) for frag in range(2)]
    for step in range(2):
        for goal_ref, out_ref in zip((own_ref, sib_ref), outs):
            for start in range(0, toks, size):
                part = pl.ds(start, size)
                goal = goal_ref[0, step, part].reshape(2 * size, width)
                first, second = (jnp.dot(take, goal, preferred_element_type=F32) for take in takes)
                for chip in range(out_ref.shape[1]):
                    for which in range(2):

                        @pl.when(core == which)
                        def _():
                            at = (2 * chip + which) * rows
                            pair = [first[:, at : at + rows], second[:, at : at + rows]]
                            out_ref[step, chip, part] = jnp.concatenate(pair, 1).astype(BF16)


def chunk_grad(scale, grad_scale, step, group, place_ref, w_refs, token_refs, goal_refs):
    w = jnp.concatenate([ref[...] for ref in w_refs], 0)
    total = None
    for x_ref, t_ref in zip(token_refs, goal_refs):
        x = x_ref[step]
        goal = jnp.concatenate([t_ref[step, place_ref[k]] for k in group], 1)
        res = (nt(x, w) * scale - goal.astype(F32)).astype(BF16)
        term = tn(res, x)
        total = term if total is None else total + term
    total = (total * grad_scale).astype(BF16)
    rows = w_refs[0].shape[0]
    return [total[i * rows : (i + 1) * rows] for i in range(len(group))]


def near_kernel(scales, group, place_ref, *refs):
    size = len(group)
    w_refs, token_refs, goal_refs = refs[:size], refs[size : size + 2], refs[size + 2 : size + 4]
    outs = refs[size + 4 :]
    for step in range(2):
        made = chunk_grad(*scales, step, group, place_ref, w_refs, token_refs, goal_refs)
        for ref, value in zip(outs[step * size :], made):
            ref[...] = value


def far_kernel(scales, near, far, place_ref, first_ref, *refs):
    size, ready = len(far), len(near)
    chips = ready + size
    w_refs, token_refs, goal_refs = refs[:size], refs[size : size + 2], refs[size + 2 : size + 4]
    near_refs, refs = refs[size + 4 : size + 4 + 2 * ready], refs[size + 4 + 2 * ready :]
    strip_refs, (weights_ref, *outs, keep_ref, send_ref, copy_ref) = refs[:chips], refs[chips:]
    made = dict(zip(near, (ref[...] for ref in near_refs[:ready])))
    made.update(zip(far, chunk_grad(*scales, 0, far, place_ref, w_refs, token_refs, goal_refs)))
    strip = tree_sum(ref[...].astype(F32) for ref in strip_refs).astype(BF16)
    for k, ref in enumerate(outs):
        rows = made[k].shape[0]
        ref[pl.ds(0, rows), :] = made[k]
        ref[pl.ds(rows, strip.shape[0]), :] = strip
    made = dict(zip(near, (ref[...] for ref in near_refs[ready:])))
    made.update(zip(far, chunk_grad(*scales, 1, far, place_ref, w_refs, token_refs, goal_refs)))
    for k in range(chips):
        (send_ref if k % 2 else keep_ref)[k // 2] = made[k]
    copy_ref[...] = jnp.where(first_ref[0] == 0, weights_ref[0], weights_ref[1])


def halve_kernel(keep_ref, got_ref, next_ref, send_ref):
    for k in range(keep_ref.shape[0]):
        total = (keep_ref[k].astype(F32) + got_ref[k].astype(F32)).astype(BF16)
        (send_ref if k % 2 else next_ref)[k // 2] = total


def gram_kernel(step, side_ref, place_ref, xo_ref, xs_ref, *refs):
    outs, scratch = refs[:-1], refs[-1]
    rows, width = outs[0].shape
    part = pl.ds(pl.multiple_of(side_ref[0] * (width // 2), width // 2), width // 2)
    total = tn(xo_ref[step, :, part], xo_ref[step]) + tn(xs_ref[step, :, part], xs_ref[step])
    scratch[...] = total.astype(BF16)
    for k, ref in enumerate(outs):
        ref[...] = scratch[pl.ds(pl.multiple_of(place_ref[k] * rows, rows), rows), :]


def add_kernel(*refs):
    refs[-1][...] = tree_sum(ref[...].astype(F32) for ref in refs[:-1]).astype(refs[-1].dtype)


def sum_kernel(place_ref, *refs):
    pieces, (grad_ref, squares_ref, gram_ref) = refs[:-3], refs[-3:]
    rows = grad_ref.shape[0]
    strip = pieces[0].shape[0] - rows
    grad = tree_sum(ref[pl.ds(0, rows), :].astype(F32) for ref in pieces)
    grad_ref[...] = grad
    squares_ref[...] = fold(grad * grad)
    for k, ref in enumerate(pieces):
        gram_ref[pl.ds(pl.multiple_of(place_ref[k] * strip, strip), strip), :] = ref[pl.ds(rows, strip), :]


def fold(x):
    rows, width = x.shape
    tiles = [x[i : i + 8] for i in range(0, rows, 8)]
    while len(tiles) > 1:
        tiles = [a + b for a, b in zip(tiles[0::2], tiles[1::2])]
    x = tiles[0]
    lanes = [x[:, i : i + 128] for i in range(0, width, 128)]
    return functools.reduce(lambda a, b: a + b, lanes)


def correct_kernel(count, factor, side_ref, *refs):
    grad_ref, squares_ref = refs[-2:]
    dw_ref, go_ref, gs_ref = refs[count : count + 3]
    half = go_ref.shape[0]
    total = tree_sum(ref[...].astype(F32) for ref in refs[:count])
    p = side_ref[0]
    extra = None
    for at, g_ref in ((p, go_ref), (1 - p, gs_ref)):
        dw = dw_ref[:, pl.ds(pl.multiple_of(at * half, half), half)]
        high = dw.astype(BF16)
        low = (dw - high.astype(F32)).astype(BF16)
        g = g_ref[...]
        term = jnp.dot(high, g, preferred_element_type=F32) + jnp.dot(
            low, g, preferred_element_type=F32
        )
        extra = term if extra is None else extra + term
    grad = total + factor * extra
    grad_ref[...] = grad
    squares_ref[...] = fold(grad * grad)


def adam(grad, norm_refs, one, two, moment_one, moment_two, weights):
    squares = jnp.sum(tree_sum(ref[...] for ref in norm_refs))
    norm = jnp.sqrt(jnp.full((1, 1), squares, F32))
    clipped = grad * jnp.minimum(1.0, clip_norm / (norm + 1e-06))
    moment_one = beta_one * moment_one + (1.0 - beta_one) * clipped
    moment_two = beta_two * moment_two + (1.0 - beta_two) * clipped * clipped
    update = moment_one / one / (jnp.sqrt(moment_two / two) + adam_eps)
    return moment_one, moment_two, weights - inner_rate * (update + decay_rate * weights)


def outer_step(theta, speed, delta):
    speed = outer_momentum * speed + delta
    return theta - outer_rate * (outer_momentum * speed + delta)


def first_kernel(
    replicas, count, first_ref, correct_ref, grad_ref, m_ref, v_ref, w_ref, outer_ref, vel_ref, total_ref, *refs
):
    norms = refs[:count]
    m_out, v_out, w_out, dw_out, theta_out, send_out = refs[count:]
    rows = grad_ref.shape[0] // 2
    first = first_ref[0]
    sends = []
    for frag in range(2):
        part = pl.ds(frag * rows, rows)
        m, v, after = adam(
            grad_ref[part, :], norms, correct_ref[0], correct_ref[1], m_ref[frag], v_ref[frag], w_ref[frag]
        )
        m_out[frag] = m
        v_out[frag] = v
        sends.append(after)
        old = outer_ref[frag]
        theta = outer_step(old, vel_ref[frag], old - total_ref[...] * (1.0 / replicas))
        now = first == frag
        theta_out[frag] = jnp.where(now, theta, old)
        after = jnp.where(now, mixing * theta + (1.0 - mixing) * after, after)
        w_out[frag] = after
        dw_out[part, :] = after.astype(BF16).astype(F32) - w_ref[frag].astype(BF16).astype(F32)
    send_out[...] = jnp.where(first == 0, sends[1], sends[0])


def last_kernel(
    replicas, count, first_ref, correct_ref, grad_ref, m_ref, v_ref, w_ref, outer_ref, vel_ref, moved_ref, *refs
):
    norms = refs[:count]
    outer_out, inner_out = refs[count:]
    rows = grad_ref.shape[0] // 2
    first = first_ref[0]
    for frag in range(2):
        part = pl.ds(frag * rows, rows)
        after = adam(
            grad_ref[part, :], norms, correct_ref[2], correct_ref[3], m_ref[frag], v_ref[frag], w_ref[frag]
        )[2]
        old = outer_ref[frag]
        theta = outer_step(old, vel_ref[frag], old - moved_ref[...] * (1.0 / replicas))
        now = first != frag
        outer_out[frag] = jnp.where(now, theta, old)
        inner_out[frag] = jnp.where(now, mixing * theta + (1.0 - mixing) * after, after)


def body(
    inner_weights,
    first_moment,
    second_moment,
    outer_weights,
    outer_velocity,
    tokens,
    targets,
    step_count,
    first_fragment,
):
    weights = inner_weights[0]
    rows, width = weights.shape[1:]
    replicas = lax.axis_size("rep")
    shards = lax.axis_size("shard")
    chips = shards // 2
    toks = tokens.shape[2]
    scale = 1.0 / math.sqrt(width)
    grad_scale = scale / (toks * shards)
    index = lax.axis_index("shard")
    core = index % 2
    chip = index // 2

    def swap(x, axis, size, by):
        return lax.ppermute(x, axis, [(i, i ^ by) for i in range(size)])

    sibling = lambda x: swap(x, "shard", shards, 1)
    across = lambda x, by: swap(x, "shard", shards, 2 * by)

    shape = jax.ShapeDtypeStruct
    block = shape((2 * rows, width), BF16)
    tile = shape((8, 128), F32)
    state = shape((2, rows, width), F32)
    row_block = shape((rows, width), F32)
    flat = shape((2 * rows, width), F32)
    side = jnp.reshape(core, (1,)).astype(jnp.int32)
    place = jnp.stack([chip ^ k for k in range(chips)]).astype(jnp.int32)

    (lowered,) = call(lower_kernel, [block], [], [weights], "lower")
    held = [lowered] + [across(lowered, k) for k in range(1, chips)]

    own_x = tokens[0]
    sib_x = sibling(own_x)

    swapped = sibling(targets)

    strip_shape = shape((width // shards, width), BF16)
    strips = call(
        functools.partial(gram_kernel, 1),
        [strip_shape] * chips,
        [side, place],
        [own_x, sib_x],
        "gram",
        [lowered],
        [pltpu.VMEM((width // 2, width), BF16)],
    )

    def spread(made):
        return [made[0]] + [across(made[k], k) for k in range(1, chips)]

    def norm_parts(squares, after):
        (both,) = call(add_kernel, [tile], [], [squares, sibling(squares)], "add_cores", after)
        return [both] + [across(both, k) for k in range(1, chips)]

    parts = shape((2, chips, toks, 2 * rows), BF16)
    own_t, sib_t = call(
        functools.partial(split_kernel, rows), [parts, parts], [side], [targets, swapped], "split", [strips[0]]
    )

    near = list(range(max(1, chips // 2)))
    far = list(range(max(1, chips // 2), chips))
    scales = (scale, grad_scale)
    made = call(
        functools.partial(near_kernel, scales, near),
        [block] * (2 * len(near)),
        [place],
        [held[k] for k in near] + [own_x, sib_x, own_t, sib_t],
        "near_grad",
    )
    pairs = shape((chips // 2, 2 * rows, width), BF16)
    *joint, keep, send, sums = call(
        functools.partial(far_kernel, scales, near, far),
        [shape((2 * rows + width // shards, width), BF16)] * chips + [pairs, pairs, row_block],
        [place, first_fragment],
        [held[k] for k in far] + [own_x, sib_x, own_t, sib_t, *made, *spread(strips), weights],
        "far_grad",
    )
    got = across(send, 1)
    pieces_one = spread(joint)

    def over_rep(x, name, after):
        by = 1
        while by < replicas:
            (x,) = call(add_kernel, [row_block], [], [x, swap(x, "rep", replicas, by)], name, after)
            by *= 2
        return x

    sums = over_rep(sums, "add_reps", [])

    grad, squares, own_g = call(
        sum_kernel,
        [flat, tile, shape((width // 2, width), BF16)],
        [place],
        pieces_one,
        "sum_pieces",
        [sums, got],
    )
    sib_g = sibling(own_g)
    norms = norm_parts(squares, [sib_g])
    bit = 2
    while bit < chips:
        half = shape((keep.shape[0] // 2, 2 * rows, width), BF16)
        keep, send = call(halve_kernel, [half, half], [], [keep, got], "halve", norms[:1])
        got = across(send, bit)
        bit *= 2
    pieces_two = [keep[0], got[0]]

    count = step_count[0].astype(F32)
    correct = jnp.stack(
        [1.0 - jnp.power(beta, count + s) for s in range(2) for beta in (beta_one, beta_two)]
    )
    m, v, middle, change, outer, moved = call(
        functools.partial(first_kernel, replicas, chips),
        [state, state, state, flat, state, row_block],
        [first_fragment, correct],
        [grad, first_moment[0], second_moment[0], weights, outer_weights, outer_velocity, sums, *norms],
        "first_update",
    )
    grad, squares = call(
        functools.partial(correct_kernel, len(pieces_two), scale * grad_scale),
        [flat, tile],
        [side],
        [*pieces_two, change, own_g, sib_g],
        "corrected",
    )
    norms = norm_parts(squares, [])
    moved = over_rep(moved, "add_moves", norms[:1])
    new_outer, new_inner = call(
        functools.partial(last_kernel, replicas, chips),
        [state, state],
        [first_fragment, correct],
        [grad, m, v, middle, outer, outer_velocity, moved, *norms],
        "last_update",
    )
    return (new_outer, new_inner[None])


def solution(mesh):
    in_specs = (
        P("rep", None, "shard", None),
        P("rep", None, "shard", None),
        P("rep", None, "shard", None),
        P(None, "shard", None),
        P(None, "shard", None),
        P("rep", None, "shard", None),
        P("rep", None, "shard", None, None),
        P(),
        P(),
    )
    out_specs = (P(None, "shard", None), P("rep", None, "shard", None))
    return jax.shard_map(body, mesh=mesh, in_specs=in_specs, out_specs=out_specs, check_vma=False)
```

```python
import functools
import math

import jax
import jax.numpy as jnp
from jax import lax
from jax.experimental import pallas as pl
from jax.experimental.pallas import tpu as pltpu
from jax.sharding import PartitionSpec as P

beta_one = 0.9
beta_two = 0.95
inner_rate = 0.1
adam_eps = 1e-08
decay_rate = 0.1
clip_norm = 0.02
outer_rate = 0.7
outer_momentum = 0.9
mixing = 0.5

F32 = jnp.float32
BF16 = jnp.bfloat16
VMEM_BYTES = 16 * 1024 * 1024


def tree_sum(items):
    items = list(items)
    while len(items) > 1:
        items = [a + b for a, b in zip(items[0::2], items[1::2])]
    return items[0]


def nt(a, b):
    return lax.dot_general(a, b, (((1,), (1,)), ((), ())), preferred_element_type=F32)


def tn(a, b):
    return lax.dot_general(a, b, (((0,), (0,)), ((), ())), preferred_element_type=F32)


def call(kernel, out_shape, scalars, arrays, name, after=(), scratch=(), flops=0):
    vmem = pl.BlockSpec(memory_space=pltpu.VMEM)

    def run(*refs):
        count = len(scalars) + len(arrays)
        kernel(*refs[:count], *refs[count + len(after) :])

    return pl.pallas_call(
        run,
        in_specs=[pl.BlockSpec(memory_space=pltpu.SMEM)] * len(scalars)
        + [vmem] * len(arrays)
        + [pl.BlockSpec(memory_space=pl.ANY)] * len(after),
        out_specs=[vmem] * len(out_shape),
        out_shape=out_shape,
        scratch_shapes=list(scratch),
        compiler_params=pltpu.CompilerParams(vmem_limit_bytes=VMEM_BYTES),
        cost_estimate=pl.CostEstimate(flops=flops, bytes_accessed=1024, transcendentals=0),
        name=name,
    )(*scalars, *arrays, *after)


def lower_kernel(w_ref, out_ref):
    rows = w_ref.shape[1]
    for frag in range(2):
        out_ref[pl.ds(frag * rows, rows), :] = w_ref[frag].astype(BF16)


def split_kernel(rows, side_ref, own_ref, sib_ref, *outs):
    core = side_ref[0]
    toks, width = own_ref.shape[2], own_ref.shape[4]
    size = math.gcd(toks, 256)
    row = lax.broadcasted_iota(jnp.int32, (size, 2 * size), 0)
    column = lax.broadcasted_iota(jnp.int32, (size, 2 * size), 1)
    takes = [(column == 2 * row + frag).astype(BF16) for frag in range(2)]
    for step in range(2):
        for goal_ref, out_ref in zip((own_ref, sib_ref), outs):
            for start in range(0, toks, size):
                part = pl.ds(start, size)
                goal = goal_ref[0, step, part].reshape(2 * size, width)
                first, second = (jnp.dot(take, goal, preferred_element_type=F32) for take in takes)
                for chip in range(out_ref.shape[1]):
                    for which in range(2):

                        @pl.when(core == which)
                        def _():
                            at = (2 * chip + which) * rows
                            pair = [first[:, at : at + rows], second[:, at : at + rows]]
                            out_ref[step, chip, part] = jnp.concatenate(pair, 1).astype(BF16)


def chunk_grad(scale, grad_scale, step, group, place_ref, w_refs, token_refs, goal_refs):
    w = jnp.concatenate([ref[...] for ref in w_refs], 0)
    total = None
    for x_ref, t_ref in zip(token_refs, goal_refs):
        x = x_ref[step]
        goal = jnp.concatenate([t_ref[step, place_ref[k]] for k in group], 1)
        res = (nt(x, w) * scale - goal.astype(F32)).astype(BF16)
        term = tn(res, x)
        total = term if total is None else total + term
    total = (total * grad_scale).astype(BF16)
    rows = w_refs[0].shape[0]
    return [total[i * rows : (i + 1) * rows] for i in range(len(group))]


def near_kernel(scales, group, place_ref, *refs):
    size = len(group)
    w_refs, token_refs, goal_refs = refs[:size], refs[size : size + 2], refs[size + 2 : size + 4]
    outs = refs[size + 4 :]
    for step in range(2):
        made = chunk_grad(*scales, step, group, place_ref, w_refs, token_refs, goal_refs)
        for ref, value in zip(outs[step * size :], made):
            ref[...] = value


def far_kernel(scales, near, far, place_ref, first_ref, *refs):
    size, ready = len(far), len(near)
    chips = ready + size
    w_refs, token_refs, goal_refs = refs[:size], refs[size : size + 2], refs[size + 2 : size + 4]
    near_refs, refs = refs[size + 4 : size + 4 + 2 * ready], refs[size + 4 + 2 * ready :]
    strip_refs, (weights_ref, *outs, keep_ref, send_ref, copy_ref) = refs[:chips], refs[chips:]
    made = dict(zip(near, (ref[...] for ref in near_refs[:ready])))
    made.update(zip(far, chunk_grad(*scales, 0, far, place_ref, w_refs, token_refs, goal_refs)))
    strip = tree_sum(ref[...].astype(F32) for ref in strip_refs).astype(BF16)
    for k, ref in enumerate(outs):
        rows = made[k].shape[0]
        ref[pl.ds(0, rows), :] = made[k]
        ref[pl.ds(rows, strip.shape[0]), :] = strip
    made = dict(zip(near, (ref[...] for ref in near_refs[ready:])))
    made.update(zip(far, chunk_grad(*scales, 1, far, place_ref, w_refs, token_refs, goal_refs)))
    for k in range(chips):
        (send_ref if k % 2 else keep_ref)[k // 2] = made[k]
    copy_ref[...] = jnp.where(first_ref[0] == 0, weights_ref[0], weights_ref[1])


def halve_kernel(keep_ref, got_ref, next_ref, send_ref):
    for k in range(keep_ref.shape[0]):
        total = (keep_ref[k].astype(F32) + got_ref[k].astype(F32)).astype(BF16)
        (send_ref if k % 2 else next_ref)[k // 2] = total


def gram_kernel(step, side_ref, place_ref, xo_ref, xs_ref, *refs):
    outs, scratch = refs[:-1], refs[-1]
    rows, width = outs[0].shape
    part = pl.ds(pl.multiple_of(side_ref[0] * (width // 2), width // 2), width // 2)
    total = tn(xo_ref[step, :, part], xo_ref[step]) + tn(xs_ref[step, :, part], xs_ref[step])
    scratch[...] = total.astype(BF16)
    for k, ref in enumerate(outs):
        ref[...] = scratch[pl.ds(pl.multiple_of(place_ref[k] * rows, rows), rows), :]


def add_kernel(*refs):
    refs[-1][...] = tree_sum(ref[...].astype(F32) for ref in refs[:-1]).astype(refs[-1].dtype)


def sum_kernel(place_ref, *refs):
    pieces, (grad_ref, squares_ref, gram_ref) = refs[:-3], refs[-3:]
    rows = grad_ref.shape[0]
    strip = pieces[0].shape[0] - rows
    grad = tree_sum(ref[pl.ds(0, rows), :].astype(F32) for ref in pieces)
    grad_ref[...] = grad
    squares_ref[...] = fold(grad * grad)
    for k, ref in enumerate(pieces):
        gram_ref[pl.ds(pl.multiple_of(place_ref[k] * strip, strip), strip), :] = ref[pl.ds(rows, strip), :]


def fold(x):
    rows, width = x.shape
    tiles = [x[i : i + 8] for i in range(0, rows, 8)]
    while len(tiles) > 1:
        tiles = [a + b for a, b in zip(tiles[0::2], tiles[1::2])]
    x = tiles[0]
    lanes = [x[:, i : i + 128] for i in range(0, width, 128)]
    return functools.reduce(lambda a, b: a + b, lanes)


def correct_kernel(count, factor, side_ref, *refs):
    grad_ref, squares_ref = refs[-2:]
    dw_ref, go_ref, gs_ref = refs[count : count + 3]
    half = go_ref.shape[0]
    total = tree_sum(ref[...].astype(F32) for ref in refs[:count])
    p = side_ref[0]
    extra = None
    for at, g_ref in ((p, go_ref), (1 - p, gs_ref)):
        dw = dw_ref[:, pl.ds(pl.multiple_of(at * half, half), half)]
        high = dw.astype(BF16)
        low = (dw - high.astype(F32)).astype(BF16)
        g = g_ref[...]
        term = jnp.dot(high, g, preferred_element_type=F32) + jnp.dot(
            low, g, preferred_element_type=F32
        )
        extra = term if extra is None else extra + term
    grad = total + factor * extra
    grad_ref[...] = grad
    squares_ref[...] = fold(grad * grad)


def adam(grad, norm_refs, one, two, moment_one, moment_two, weights):
    squares = jnp.sum(tree_sum(ref[...] for ref in norm_refs))
    norm = jnp.sqrt(jnp.full((1, 1), squares, F32))
    clipped = grad * jnp.minimum(1.0, clip_norm / (norm + 1e-06))
    moment_one = beta_one * moment_one + (1.0 - beta_one) * clipped
    moment_two = beta_two * moment_two + (1.0 - beta_two) * clipped * clipped
    update = moment_one / one / (jnp.sqrt(moment_two / two) + adam_eps)
    return moment_one, moment_two, weights - inner_rate * (update + decay_rate * weights)


def outer_step(theta, speed, delta):
    speed = outer_momentum * speed + delta
    return theta - outer_rate * (outer_momentum * speed + delta)


def first_kernel(
    replicas, count, first_ref, correct_ref, grad_ref, m_ref, v_ref, w_ref, outer_ref, vel_ref, total_ref, *refs
):
    norms = refs[:count]
    m_out, v_out, w_out, dw_out, theta_out, send_out = refs[count:]
    rows = grad_ref.shape[0] // 2
    first = first_ref[0]
    sends = []
    for frag in range(2):
        part = pl.ds(frag * rows, rows)
        m, v, after = adam(
            grad_ref[part, :], norms, correct_ref[0], correct_ref[1], m_ref[frag], v_ref[frag], w_ref[frag]
        )
        m_out[frag] = m
        v_out[frag] = v
        sends.append(after)
        old = outer_ref[frag]
        theta = outer_step(old, vel_ref[frag], old - total_ref[...] * (1.0 / replicas))
        now = first == frag
        theta_out[frag] = jnp.where(now, theta, old)
        after = jnp.where(now, mixing * theta + (1.0 - mixing) * after, after)
        w_out[frag] = after
        dw_out[part, :] = after.astype(BF16).astype(F32) - w_ref[frag].astype(BF16).astype(F32)
    send_out[...] = jnp.where(first == 0, sends[1], sends[0])


def last_kernel(
    replicas, count, first_ref, correct_ref, grad_ref, m_ref, v_ref, w_ref, outer_ref, vel_ref, moved_ref, *refs
):
    norms = refs[:count]
    outer_out, inner_out = refs[count:]
    rows = grad_ref.shape[0] // 2
    first = first_ref[0]
    for frag in range(2):
        part = pl.ds(frag * rows, rows)
        after = adam(
            grad_ref[part, :], norms, correct_ref[2], correct_ref[3], m_ref[frag], v_ref[frag], w_ref[frag]
        )[2]
        old = outer_ref[frag]
        theta = outer_step(old, vel_ref[frag], old - moved_ref[...] * (1.0 / replicas))
        now = first != frag
        outer_out[frag] = jnp.where(now, theta, old)
        inner_out[frag] = jnp.where(now, mixing * theta + (1.0 - mixing) * after, after)


def body(
    inner_weights,
    first_moment,
    second_moment,
    outer_weights,
    outer_velocity,
    tokens,
    targets,
    step_count,
    first_fragment,
):
    weights = inner_weights[0]
    rows, width = weights.shape[1:]
    replicas = lax.axis_size("rep")
    shards = lax.axis_size("shard")
    chips = shards // 2
    toks = tokens.shape[2]
    scale = 1.0 / math.sqrt(width)
    grad_scale = scale / (toks * shards)
    index = lax.axis_index("shard")
    core = index % 2
    chip = index // 2

    def swap(x, axis, size, by):
        return lax.ppermute(x, axis, [(i, i ^ by) for i in range(size)])

    sibling = lambda x: swap(x, "shard", shards, 1)
    across = lambda x, by: swap(x, "shard", shards, 2 * by)

    shape = jax.ShapeDtypeStruct
    block = shape((2 * rows, width), BF16)
    tile = shape((8, 128), F32)
    state = shape((2, rows, width), F32)
    row_block = shape((rows, width), F32)
    flat = shape((2 * rows, width), F32)
    side = jnp.reshape(core, (1,)).astype(jnp.int32)
    place = jnp.stack([chip ^ k for k in range(chips)]).astype(jnp.int32)

    (lowered,) = call(lower_kernel, [block], [], [weights], "lower")
    held = [lowered] + [across(lowered, k) for k in range(1, chips)]

    own_x = tokens[0]
    sib_x = sibling(own_x)

    swapped = sibling(targets)

    strip_shape = shape((width // shards, width), BF16)
    strips = call(
        functools.partial(gram_kernel, 1),
        [strip_shape] * chips,
        [side, place],
        [own_x, sib_x],
        "gram",
        [lowered],
        [pltpu.VMEM((width // 2, width), BF16)],
    )

    def spread(made):
        return [made[0]] + [across(made[k], k) for k in range(1, chips)]

    def norm_parts(squares, after):
        (both,) = call(add_kernel, [tile], [], [squares, sibling(squares)], "add_cores", after)
        return [both] + [across(both, k) for k in range(1, chips)]

    parts = shape((2, chips, toks, 2 * rows), BF16)
    own_t, sib_t = call(
        functools.partial(split_kernel, rows), [parts, parts], [side], [targets, swapped], "split", [strips[0]]
    )

    near = list(range(max(1, chips // 2)))
    far = list(range(max(1, chips // 2), chips))
    scales = (scale, grad_scale)
    made = call(
        functools.partial(near_kernel, scales, near),
        [block] * (2 * len(near)),
        [place],
        [held[k] for k in near] + [own_x, sib_x, own_t, sib_t],
        "near_grad",
    )
    pairs = shape((chips // 2, 2 * rows, width), BF16)
    *joint, keep, send, sums = call(
        functools.partial(far_kernel, scales, near, far),
        [shape((2 * rows + width // shards, width), BF16)] * chips + [pairs, pairs, row_block],
        [place, first_fragment],
        [held[k] for k in far] + [own_x, sib_x, own_t, sib_t, *made, *spread(strips), weights],
        "far_grad",
    )
    got = across(send, 1)
    pieces_one = spread(joint)

    def over_rep(x, name, after):
        by = 1
        while by < replicas:
            (x,) = call(add_kernel, [row_block], [], [x, swap(x, "rep", replicas, by)], name, after)
            by *= 2
        return x

    sums = over_rep(sums, "add_reps", [])

    grad, squares, own_g = call(
        sum_kernel,
        [flat, tile, shape((width // 2, width), BF16)],
        [place],
        pieces_one,
        "sum_pieces",
        [sums],
    )
    sib_g = sibling(own_g)
    norms = norm_parts(squares, [sib_g, got])
    bit = 2
    while bit < chips:
        half = shape((keep.shape[0] // 2, 2 * rows, width), BF16)
        keep, send = call(halve_kernel, [half, half], [], [keep, got], "halve", norms[:1])
        got = across(send, bit)
        bit *= 2
    pieces_two = [keep[0], got[0]]

    count = step_count[0].astype(F32)
    correct = jnp.stack(
        [1.0 - jnp.power(beta, count + s) for s in range(2) for beta in (beta_one, beta_two)]
    )
    m, v, middle, change, outer, moved = call(
        functools.partial(first_kernel, replicas, chips),
        [state, state, state, flat, state, row_block],
        [first_fragment, correct],
        [grad, first_moment[0], second_moment[0], weights, outer_weights, outer_velocity, sums, *norms],
        "first_update",
    )
    grad, squares = call(
        functools.partial(correct_kernel, len(pieces_two), scale * grad_scale),
        [flat, tile],
        [side],
        [*pieces_two, change, own_g, sib_g],
        "corrected",
    )
    norms = norm_parts(squares, [])
    moved = over_rep(moved, "add_moves", norms[:1])
    new_outer, new_inner = call(
        functools.partial(last_kernel, replicas, chips),
        [state, state],
        [first_fragment, correct],
        [grad, m, v, middle, outer, outer_velocity, moved, *norms],
        "last_update",
    )
    return (new_outer, new_inner[None])


def solution(mesh):
    in_specs = (
        P("rep", None, "shard", None),
        P("rep", None, "shard", None),
        P("rep", None, "shard", None),
        P(None, "shard", None),
        P(None, "shard", None),
        P("rep", None, "shard", None),
        P("rep", None, "shard", None, None),
        P(),
        P(),
    )
    out_specs = (P(None, "shard", None), P("rep", None, "shard", None))
    return jax.shard_map(body, mesh=mesh, in_specs=in_specs, out_specs=out_specs, check_vma=False)
```
